32 devices in a mesh: seq: 16 (over z, y, x), head: 2 (over core).
Axes of the slice: x: 2, y: 2, z: 4, core: 2. Of those that a mesh axis runs over, the one named last changes fastest.
Arguments:
- queries: bfloat16 [2048, 512], P('seq', 'head')
- keys_values: bfloat16 [2048, 256], P(('seq', 'head'))
- selected: int32 [16, 3], replicated, may hold values from -1 to 3, as said below
Outputs:
- attended: bfloat16 [2048, 512], P('seq', 'head')
The draws below stay inside these ranges and needn't reach their ends.
Inputs may be any that keep to these rules, and one draw needn't show every extreme that they name: selected[c, 0] = c // 4, the span's own block; selected[c, 1] and selected[c, 2] are two different blocks before it, chosen at random; where fewer than two earlier blocks exist, the missing entries are -1 (column 1 first filled).
All inputs are finite; a program needn't handle non-finite values.
Results may differ from the reference program's by a relative error of at most 0.0052.
Values may be sent and summed in bfloat16 or wider, within the bound.
No kernel may reach another device: no remote copies, remote signals or barrier semaphores. Data moves between devices by JAX's collectives and lax.ppermute only.
A program may use at most 64 MiB of HBM per device.

```python
import jax
import jax.numpy as jnp
from jax import lax

DH = 128
HQ = 4
TOK_DEV = 128
GROUP = 4
TOPK = 3
BLOCK = 512
TOKENS = 2048
N_SEQ = 16


def shared_keys(key):
    return jax.random.normal(jax.random.fold_in(key, 11), (TOKENS, 2 * DH), jnp.float32)


def draw_keys_values(key, part):
    return shared_keys(key).astype(jnp.bfloat16)


def draw_queries(key, part):
    normal_rows = jax.random.normal(jax.random.fold_in(key, 23), (TOKENS, HQ * DH), jnp.float32)
    return normal_rows.astype(jnp.bfloat16)


def draw_selected(key, part):
    spans = jnp.arange(N_SEQ, dtype=jnp.int32)
    own_block = spans // GROUP
    first_bits = jax.random.randint(jax.random.fold_in(key, 31), (N_SEQ,), 0, 1 << 20, dtype=jnp.int32)
    second_bits = jax.random.randint(jax.random.fold_in(key, 37), (N_SEQ,), 0, 1 << 20, dtype=jnp.int32)
    first = first_bits % jnp.maximum(own_block, 1)
    second = second_bits % jnp.maximum(own_block - 1, 1)
    second = second + (second >= first).astype(jnp.int32)
    column_one = jnp.where(own_block >= 1, first, -1)
    column_two = jnp.where(own_block >= 2, second, -1)
    return jnp.stack([own_block, column_one, column_two], axis=1).astype(jnp.int32)


def setup_inputs(seed: int = 0) -> dict:
    splits = jax.random.split(jax.random.key(seed), 4)
    queries = draw_queries(jax.random.fold_in(splits[3], 71), 0)
    keys_values = draw_keys_values(jax.random.fold_in(splits[3], 71), 0)
    selected = draw_selected(jax.random.fold_in(splits[3], 71), 0)
    return {"queries": queries, "keys_values": keys_values, "selected": selected}


def part_attend(query_rows, block_kv, query_pos, key_pos):
    keys = block_kv[:, :DH]
    values = block_kv[:, DH:]
    scores = jnp.einsum("nhd,kd->hnk", query_rows, keys) * (DH ** -0.5)
    allowed = key_pos[None, :] <= query_pos[:, None]
    scores = jnp.where(allowed[None], scores, -1e30)
    top = jnp.max(scores, axis=-1)
    expo = jnp.exp(scores - top[..., None])
    total = jnp.sum(expo, axis=-1)
    weights = expo.astype(jnp.bfloat16).astype(jnp.float32)
    outputs = jnp.einsum("hnk,kd->nhd", weights, values) / jnp.transpose(total)[..., None]
    lse = jnp.transpose(top + jnp.log(total))
    return outputs, lse


def reference(queries, keys_values, selected):
    kv_all = keys_values.astype(jnp.float32)

    def one_span(span):
        start = (span * TOK_DEV).astype(jnp.int32)
        rows = lax.dynamic_slice_in_dim(queries, start, TOK_DEV, 0).astype(jnp.float32)
        rows = rows.reshape(TOK_DEV, HQ, DH)
        query_pos = start + jnp.arange(TOK_DEV, dtype=jnp.int32)
        outs_list = []
        lse_list = []
        for column in range(TOPK):
            block_id = selected[span, column]
            safe = jnp.maximum(block_id, 0).astype(jnp.int32)
            kv_start = (safe * BLOCK).astype(jnp.int32)
            block_kv = lax.dynamic_slice_in_dim(kv_all, kv_start, BLOCK, 0)
            key_pos = kv_start + jnp.arange(BLOCK, dtype=jnp.int32)
            outputs, lse = part_attend(rows, block_kv, query_pos, key_pos)
            if column >= 1:
                outputs = lax.optimization_barrier(outputs.astype(jnp.bfloat16)).astype(jnp.float32)
            lse = jnp.where(block_id >= 0, lse, -1e30)
            outs_list.append(outputs)
            lse_list.append(lse)
        lse_all = jnp.stack(lse_list)
        outs_all = jnp.stack(outs_list)
        largest = jnp.max(lse_all, axis=0)
        scale = jnp.exp(lse_all - largest[None])
        merged = jnp.sum(scale[..., None] * outs_all, axis=0) / jnp.sum(scale, axis=0)[..., None]
        return merged.reshape(TOK_DEV, HQ * DH).astype(jnp.bfloat16)

    result = lax.map(one_span, jnp.arange(N_SEQ, dtype=jnp.int32))
    return result.reshape(TOKENS, HQ * DH)
```

```python
import functools

import jax
import jax.numpy as jnp
from jax import lax
from jax.experimental import pallas as pl
from jax.experimental.pallas import tpu as pltpu
from jax.sharding import PartitionSpec as P

DH = 128
GROUP = 4
TOPK = 3
LOG2E = 1.4426950408889634
LOW = -3e38


def swapped(rows, axis, step):
    count = lax.axis_size(axis)
    return lax.ppermute(rows, axis, [(i, i ^ step) for i in range(count)])


def pick_kernel(blocks, me_ref, selected_ref, *refs):
    held, messages = refs[:blocks], refs[blocks:]
    rows = held[0].shape[0]
    me = me_ref[0]
    mine = me // GROUP
    for step in range(GROUP):
        messages[step][0:rows, :] = held[0][...]
        for column in range(1, TOPK):
            wanted = jnp.maximum(selected_ref[me ^ step, column], 0) ^ mine
            for index in range(blocks):

                @pl.when(wanted == index)
                def _():
                    messages[step][column * rows : (column + 1) * rows, :] = held[index][...]


def pick(me, selected, held):
    rows, width = held[0].shape
    message = jax.ShapeDtypeStruct((TOPK * rows, width), held[0].dtype)
    smem = pl.BlockSpec(memory_space=pltpu.SMEM)
    vmem = pl.BlockSpec(memory_space=pltpu.VMEM)
    return pl.pallas_call(
        functools.partial(pick_kernel, len(held)),
        out_shape=[message] * GROUP,
        in_specs=[smem, smem] + [vmem] * len(held),
        out_specs=[vmem] * GROUP,
        name="pick",
    )(me, selected, *held)


def attend_kernel(where_ref, selected_ref, queries_ref, *refs):
    pieces, out_ref = refs[:-1], refs[-1]
    tokens, width = queries_ref.shape
    heads = width // DH
    length = pieces[0].shape[0]
    rows = length // TOPK
    me, head = where_ref[0], where_ref[1]
    part = me % GROUP
    queries = queries_ref[...]
    stacked = jnp.concatenate([queries[:, h * DH : (h + 1) * DH] for h in range(heads)], axis=0)
    kv = jnp.concatenate([piece[...] for piece in pieces], axis=0)
    scores = lax.dot_general(
        stacked, kv[:, :DH], (((1,), (1,)), ((), ())), preferred_element_type=jnp.float32
    ) * (DH ** (-0.5) * LOG2E)
    lane = lax.broadcasted_iota(jnp.int32, (1, length), 1)
    firsts = []
    for index in range(len(pieces)):
        step, other = index % GROUP, index // GROUP
        position = (part ^ step) * tokens + (head ^ other) * rows + lane
        one = jnp.where(selected_ref[me, 1] >= 0, 0, GROUP * tokens)
        two = jnp.where(selected_ref[me, 2] >= 0, 0, GROUP * tokens)
        firsts.append(jnp.where(lane < rows, position, jnp.where(lane < 2 * rows, one, two)))
    first = jnp.concatenate(firsts, axis=1)
    token = lax.broadcasted_iota(jnp.int32, (heads * tokens, 1), 0) % tokens
    scores = jnp.where(first <= part * tokens + token, scores, LOW)
    top = jnp.max(scores, axis=1, keepdims=True)
    weights = jnp.exp2(scores - top)
    total = jnp.sum(weights, axis=1, keepdims=True)
    out = jnp.dot(weights.astype(jnp.bfloat16), kv[:, DH:], preferred_element_type=jnp.float32) / total
    for h in range(heads):
        out_ref[:, h * DH : (h + 1) * DH] = out[h * tokens : (h + 1) * tokens].astype(out_ref.dtype)


def attend(where, selected, queries, pieces):
    smem = pl.BlockSpec(memory_space=pltpu.SMEM)
    vmem = pl.BlockSpec(memory_space=pltpu.VMEM)
    return pl.pallas_call(
        attend_kernel,
        out_shape=jax.ShapeDtypeStruct(queries.shape, queries.dtype),
        in_specs=[smem, smem] + [vmem] * (1 + len(pieces)),
        out_specs=vmem,
        name="attend",
    )(where, selected, queries, *pieces)


def shards(queries, keys_values, selected):
    blocks = lax.axis_size("seq") // GROUP
    me = lax.axis_index("seq").astype(jnp.int32)
    head = lax.axis_index("head").astype(jnp.int32)
    held = {0: keys_values}
    for step in range(blocks - 1, 0, -1):
        held[step] = swapped(keys_values, "seq", step * GROUP)
    own = pick(me[None], selected, [held[step] for step in range(blocks)])
    near = [own[0]] + [None] * (GROUP - 1)
    for step in (3, 1, 2):
        near[step] = swapped(own[step], "seq", step)
    far = [swapped(piece, "head", 1) for piece in near]
    return attend(jnp.stack([me, head]), selected, queries, near + far)


def solution(mesh):
    in_specs = (P("seq", "head"), P(("seq", "head"), None), P())
    out_specs = P("seq", "head")
    return jax.shard_map(shards, mesh=mesh, in_specs=in_specs, out_specs=out_specs, check_vma=False)
```

```python
import functools

import jax
import jax.numpy as jnp
from jax import lax
from jax.experimental import pallas as pl
from jax.experimental.pallas import tpu as pltpu
from jax.sharding import PartitionSpec as P

DH = 128
GROUP = 4
TOPK = 3
LOG2E = 1.4426950408889634
LOW = -3e38
VMEM = 16 << 20


def swapped(rows, axis, step):
    count = lax.axis_size(axis)
    return lax.ppermute(rows, axis, [(i, i ^ step) for i in range(count)])


def kernel_call(body, out_shape, name, smem, vmem):
    return pl.pallas_call(
        body,
        out_shape=out_shape,
        in_specs=[pl.BlockSpec(memory_space=pltpu.SMEM)] * len(smem)
        + [pl.BlockSpec(memory_space=pltpu.VMEM)] * len(vmem),
        out_specs=jax.tree.map(lambda _: pl.BlockSpec(memory_space=pltpu.VMEM), out_shape),
        compiler_params=pltpu.CompilerParams(vmem_limit_bytes=VMEM),
        name=name,
    )(*smem, *vmem)


def pick_kernel(columns, blocks, selected_ref, *refs):
    held, messages = refs[:blocks], refs[blocks:]
    rows = held[0].shape[0]
    me = lax.axis_index("seq")
    mine = me // GROUP
    for step in range(GROUP):
        messages[step][0:rows, :] = held[0][...]
        for column in range(1, columns):
            wanted = selected_ref[me ^ step, column] ^ mine
            for index in range(1, blocks):

                @pl.when(wanted == index)
                def _():
                    messages[step][column * rows : (column + 1) * rows, :] = held[index][...]


def pick(columns, selected, held):
    rows, width = held[0].shape
    message = jax.ShapeDtypeStruct((columns * rows, width), held[0].dtype)
    body = functools.partial(pick_kernel, columns, len(held))
    return kernel_call(body, [message] * GROUP, f"pick_{columns}", [selected], held)


def attend_kernel(columns, queries_ref, *refs):
    pieces, out_ref = refs[:-1], refs[-1]
    tokens, width = queries_ref.shape
    heads = width // DH
    length = pieces[0].shape[0]
    rows = length // columns
    part = lax.axis_index("seq") % GROUP
    head = lax.axis_index("head")
    queries = queries_ref[...]
    stacked = jnp.concatenate([queries[:, h * DH : (h + 1) * DH] for h in range(heads)], axis=0)
    kv = jnp.concatenate([piece[...] for piece in pieces], axis=0)
    scores = lax.dot_general(
        stacked, kv[:, :DH], (((1,), (1,)), ((), ())), preferred_element_type=jnp.float32
    ) * (DH ** (-0.5) * LOG2E)
    lane = lax.broadcasted_iota(jnp.int32, (1, length), 1)
    positions = []
    for index in range(len(pieces)):
        step, other = index % GROUP, index // GROUP
        position = (part ^ step) * tokens + (head ^ other) * rows + lane
        positions.append(jnp.where(lane < rows, position, 0))
    position = jnp.concatenate(positions, axis=1)
    token = lax.broadcasted_iota(jnp.int32, (heads * tokens, 1), 0) % tokens
    scores = jnp.where(position <= part * tokens + token, scores, LOW)
    top = jnp.max(scores, axis=1, keepdims=True)
    weights = jnp.exp2(scores - top)
    total = jnp.sum(weights, axis=1, keepdims=True)
    out = jnp.dot(weights.astype(jnp.bfloat16), kv[:, DH:], preferred_element_type=jnp.float32) / total
    for h in range(heads):
        out_ref[:, h * DH : (h + 1) * DH] = out[h * tokens : (h + 1) * tokens].astype(out_ref.dtype)


def attend(columns, queries, pieces):
    out = jax.ShapeDtypeStruct(queries.shape, queries.dtype)
    body = functools.partial(attend_kernel, columns)
    return kernel_call(body, out, f"attend_{columns}", [], [queries] + pieces)


def plane(columns, queries, selected, held):
    own = [held[0]] * GROUP if columns == 1 else pick(columns, selected, held)
    near = [own[0]] + [None] * (GROUP - 1)
    for step in (3, 1, 2):
        near[step] = swapped(own[step], "seq", step)
    far = [swapped(piece, "head", 1) for piece in near]
    return attend(columns, queries, near + far)


def shards(queries, keys_values, selected):
    blocks = lax.axis_size("seq") // GROUP
    mine = lax.axis_index("seq") // GROUP
    held = {0: keys_values}
    for step in range(blocks - 1, 0, -1):
        held[step] = swapped(keys_values, "seq", step * GROUP)
    held = [held[step] for step in range(blocks)]
    branches = [functools.partial(plane, columns) for columns in range(1, TOPK + 1)]
    return lax.switch(jnp.minimum(mine, TOPK - 1), branches, queries, selected, held)


def solution(mesh):
    in_specs = (P("seq", "head"), P(("seq", "head"), None), P())
    out_specs = P("seq", "head")
    return jax.shard_map(shards, mesh=mesh, in_specs=in_specs, out_specs=out_specs, check_vma=False)
```

```python
import functools

import jax
import jax.numpy as jnp
from jax import lax
from jax.experimental import pallas as pl
from jax.experimental.pallas import tpu as pltpu
from jax.sharding import PartitionSpec as P

DH = 128
GROUP = 4
TOPK = 3
LOG2E = 1.4426950408889634
LOW = -3e38
VMEM = 16 << 20


def swapped(rows, axis, step):
    count = lax.axis_size(axis)
    return lax.ppermute(rows, axis, [(i, i ^ step) for i in range(count)])


def kernel_call(body, out_shape, name, smem, vmem):
    return pl.pallas_call(
        body,
        out_shape=out_shape,
        in_specs=[pl.BlockSpec(memory_space=pltpu.SMEM)] * len(smem)
        + [pl.BlockSpec(memory_space=pltpu.VMEM)] * len(vmem),
        out_specs=jax.tree.map(lambda _: pl.BlockSpec(memory_space=pltpu.VMEM), out_shape),
        compiler_params=pltpu.CompilerParams(vmem_limit_bytes=VMEM),
        name=name,
    )(*smem, *vmem)


def join_kernel(*refs):
    rows = refs[0].shape[0]
    for index, piece in enumerate(refs[:-1]):
        refs[-1][index * rows : (index + 1) * rows, :] = piece[...]


def join(pieces):
    rows, width = pieces[0].shape
    out = jax.ShapeDtypeStruct((len(pieces) * rows, width), pieces[0].dtype)
    return kernel_call(join_kernel, out, "join", [], pieces)


def pick_kernel(columns, blocks, selected_ref, *refs):
    held, messages = refs[:blocks], refs[blocks:]
    rows = held[0].shape[0]
    me = lax.axis_index("seq")
    mine = me // GROUP
    for step in range(GROUP):
        messages[step][0:rows, :] = held[0][...]
        for column in range(1, columns):
            start = column * rows
            if columns == 2:
                messages[step][start : start + rows, :] = held[1][...]
                continue
            wanted = selected_ref[me ^ step, column] ^ mine
            for index in range(1, blocks):

                @pl.when(wanted == index)
                def _():
                    messages[step][start : start + rows, :] = held[index][...]


def pick(columns, selected, held):
    rows, width = held[0].shape
    messages = [jax.ShapeDtypeStruct((columns * rows, width), held[0].dtype)] * GROUP
    body = functools.partial(pick_kernel, columns, len(held))
    return kernel_call(body, messages, f"pick_{columns}", [selected], held)


def attend_kernel(rows, places, queries_ref, *refs):
    pieces, out_ref = refs[:-1], refs[-1]
    tokens, width = queries_ref.shape
    heads = width // DH
    part = lax.axis_index("seq") % GROUP
    head = lax.axis_index("head")
    queries = queries_ref[...]
    stacked = jnp.concatenate([queries[:, h * DH : (h + 1) * DH] for h in range(heads)], axis=0)
    kv = jnp.concatenate([piece[...] for piece in pieces], axis=0)
    scores = lax.dot_general(
        stacked, kv[:, :DH], (((1,), (1,)), ((), ())), preferred_element_type=jnp.float32
    ) * (DH ** (-0.5) * LOG2E)
    positions = []
    for piece, place in zip(pieces, places):
        lane = lax.broadcasted_iota(jnp.int32, (1, piece.shape[0]), 1)
        step, other = place
        position = (part ^ step) * tokens + (head ^ other) * rows + lane
        positions.append(jnp.where(lane < rows, position, 0))
    position = jnp.concatenate(positions, axis=1)
    token = lax.broadcasted_iota(jnp.int32, (heads * tokens, 1), 0) % tokens
    scores = jnp.where(position <= part * tokens + token, scores, LOW)
    top = jnp.max(scores, axis=1, keepdims=True)
    weights = jnp.exp2(scores - top)
    total = jnp.sum(weights, axis=1, keepdims=True)
    out = jnp.dot(weights.astype(jnp.bfloat16), kv[:, DH:], preferred_element_type=jnp.float32) / total
    for h in range(heads):
        out_ref[:, h * DH : (h + 1) * DH] = out[h * tokens : (h + 1) * tokens].astype(out_ref.dtype)


def attend(rows, queries, placed):
    out = jax.ShapeDtypeStruct(queries.shape, queries.dtype)
    places, pieces = zip(*placed)
    body = functools.partial(attend_kernel, rows, places)
    return kernel_call(body, out, f"attend_{len(pieces)}", [], [queries, *pieces])


def first_block(queries, rows):
    diagonal = swapped(rows, "seq", 3)
    beside = swapped(rows, "seq", 1)
    diagonal, again = lax.optimization_barrier((diagonal, rows))
    near = join([rows, beside, swapped(again, "seq", 2), diagonal])
    far = swapped(near, "head", 1)
    length = rows.shape[0]
    placed = []
    for other, piece in enumerate((near, far)):
        for step in range(GROUP):
            placed.append(((step, other), piece[step * length : (step + 1) * length]))
    return attend(length, queries, placed)


def later_block(columns, queries, selected, held):
    own = pick(columns, selected, held)
    near = [own[0]] + [None] * (GROUP - 1)
    for step in (3, 1, 2):
        near[step] = swapped(own[step], "seq", step)
    far = [swapped(piece, "head", 1) for piece in near]
    placed = []
    for step in range(GROUP):
        placed += [((step, 0), near[step]), ((step, 1), far[step])]
    return attend(held[0].shape[0], queries, placed)


def shards(queries, keys_values, selected):
    blocks = lax.axis_size("seq") // GROUP
    mine = lax.axis_index("seq") // GROUP
    held = {0: keys_values}
    for step in range(blocks - 1, 0, -1):
        held[step] = swapped(keys_values, "seq", step * GROUP)
    held = [held[step] for step in range(blocks)]
    level = jnp.minimum(mine, TOPK - 1)
    first = lax.cond(
        level == 0,
        lambda: first_block(queries, keys_values),
        lambda: jnp.zeros_like(queries),
    )
    branches = [functools.partial(later_block, columns) for columns in range(2, TOPK + 1)]
    return lax.switch(level, [lambda *_: first] + branches, queries, selected, held)


def solution(mesh):
    in_specs = (P("seq", "head"), P(("seq", "head"), None), P())
    out_specs = P("seq", "head")
    return jax.shard_map(shards, mesh=mesh, in_specs=in_specs, out_specs=out_specs, check_vma=False)
```

```python
import functools

import jax
import jax.numpy as jnp
from jax import lax
from jax.experimental import pallas as pl
from jax.experimental.pallas import tpu as pltpu
from jax.sharding import PartitionSpec as P

DH = 128
GROUP = 4
TOPK = 3
LOG2E = 1.4426950408889634
LOW = -3e38
VMEM = 16 << 20


def swapped(rows, axis, step):
    count = lax.axis_size(axis)
    return lax.ppermute(rows, axis, [(i, i ^ step) for i in range(count)])


def kernel_call(body, out_shape, name, arrays):
    vmem = pl.BlockSpec(memory_space=pltpu.VMEM)
    return pl.pallas_call(
        body,
        out_shape=out_shape,
        in_specs=[vmem] * len(arrays),
        out_specs=jax.tree.map(lambda _: vmem, out_shape),
        compiler_params=pltpu.CompilerParams(vmem_limit_bytes=VMEM),
        name=name,
    )(*arrays)


def join_kernel(*refs):
    rows = refs[0].shape[0]
    for index, piece in enumerate(refs[:-1]):
        refs[-1][index * rows : (index + 1) * rows, :] = piece[...]


def join(pieces):
    rows, width = pieces[0].shape
    out = jax.ShapeDtypeStruct((len(pieces) * rows, width), pieces[0].dtype)
    return kernel_call(join_kernel, out, "join", pieces)


def pick_kernel(columns, blocks, selected_ref, *refs):
    held, messages = refs[:blocks], refs[blocks:]
    rows = held[0].shape[0]
    me = lax.axis_index("seq")
    mine = me // GROUP
    for step in range(GROUP):
        messages[step][0:rows, :] = held[0][...]
        for column in range(1, columns):
            picked = held[1][...]
            if columns > 2:
                wanted = selected_ref[pl.ds(me ^ step, 1), column : column + 1] ^ mine
                wanted = jnp.broadcast_to(wanted, picked.shape)
                for index in range(2, blocks):
                    picked = jnp.where(wanted == index, held[index][...], picked)
            messages[step][column * rows : (column + 1) * rows, :] = picked


def pick(columns, selected, held):
    rows, width = held[0].shape
    messages = [jax.ShapeDtypeStruct((columns * rows, width), held[0].dtype)] * GROUP
    body = functools.partial(pick_kernel, columns, len(held))
    return kernel_call(body, messages, f"pick_{columns}", [selected, *held])


def attend_kernel(rows, places, resumed, last, queries_ref, *refs):
    pieces, rest = refs[: len(places)], refs[len(places) :]
    state, outs = (rest[:3], rest[3:]) if resumed else ((), rest)
    tokens, width = queries_ref.shape
    heads = width // DH
    part = lax.axis_index("seq") % GROUP
    head = lax.axis_index("head")
    queries = queries_ref[...]
    stacked = jnp.concatenate([queries[:, h * DH : (h + 1) * DH] for h in range(heads)], axis=0)
    parts = [piece[:rows, :] for piece in pieces]
    parts += [piece[rows:, :] for piece in pieces if piece.shape[0] > rows]
    kv = jnp.concatenate(parts, axis=0)
    scores = lax.dot_general(
        stacked, kv[:, :DH], (((1,), (1,)), ((), ())), preferred_element_type=jnp.float32
    ) * (DH ** (-0.5) * LOG2E)
    edge = min(-(-len(pieces) * rows // DH) * DH, kv.shape[0])
    lane = lax.broadcasted_iota(jnp.int32, (1, edge), 1)
    position = jnp.zeros_like(lane)
    for index, (step, other) in enumerate(places):
        start = (part ^ step) * tokens + (head ^ other) * rows - index * rows
        inside = (lane >= index * rows) & (lane < (index + 1) * rows)
        position = jnp.where(inside, start + lane, position)
    token = lax.broadcasted_iota(jnp.int32, (heads * tokens, 1), 0) % tokens
    own = jnp.where(position <= part * tokens + token, scores[:, :edge], LOW)
    scores = jnp.concatenate([own, scores[:, edge:]], axis=1) if edge < kv.shape[0] else own
    top = jnp.max(scores, axis=1, keepdims=True)
    if resumed:
        before = state[0][:, :1]
        top = jnp.maximum(top, before)
    weights = jnp.exp2(scores - top)
    total = jnp.sum(weights, axis=1, keepdims=True)
    out = jnp.dot(weights.astype(jnp.bfloat16), kv[:, DH:], preferred_element_type=jnp.float32)
    if resumed:
        scale = jnp.exp2(before - top)
        total += scale * state[1][:, :1]
        out += scale * state[2][...]
    if not last:
        outs[0][...] = jnp.broadcast_to(top, outs[0].shape)
        outs[1][...] = jnp.broadcast_to(total, outs[1].shape)
        outs[2][...] = out
        return
    out /= total
    for h in range(heads):
        outs[0][:, h * DH : (h + 1) * DH] = out[h * tokens : (h + 1) * tokens].astype(outs[0].dtype)


def attend(rows, queries, placed, state=(), last=True):
    tokens, width = queries.shape
    running = jax.ShapeDtypeStruct((tokens * width // DH, DH), jnp.float32)
    out = jax.ShapeDtypeStruct(queries.shape, queries.dtype) if last else [running] * 3
    places, pieces = zip(*placed)
    body = functools.partial(attend_kernel, rows, places, bool(state), last)
    return kernel_call(body, out, f"attend_{len(pieces)}", [queries, *pieces, *state])


def first_block(queries, rows):
    diagonal = swapped(rows, "seq", 3)
    beside = swapped(rows, "seq", 1)
    diagonal, again = lax.optimization_barrier((diagonal, rows))
    near = join([rows, beside, swapped(again, "seq", 2), diagonal])
    far = swapped(near, "head", 1)
    length = rows.shape[0]
    placed = []
    for other, piece in enumerate((near, far)):
        for step in range(GROUP):
            placed.append(((step, other), piece[step * length : (step + 1) * length]))
    return attend(length, queries, placed)


def later_block(columns, queries, selected, held):
    own = pick(columns, selected, held)
    near = [own[0]] + [None] * (GROUP - 1)
    for step in (3, 1, 2):
        near[step] = swapped(own[step], "seq", step)
    far = [swapped(piece, "head", 1) for piece in near]
    length = held[0].shape[0]
    placed = []
    for step in (0, 3, 1, 2):
        placed += [((step, 0), near[step]), ((step, 1), far[step])]
    state = attend(length, queries, placed[:4], last=False)
    state = attend(length, queries, placed[4:7], state, last=False)
    return attend(length, queries, placed[7:], state)


def shards(queries, keys_values, selected):
    blocks = lax.axis_size("seq") // GROUP
    mine = lax.axis_index("seq") // GROUP
    held = {0: keys_values}
    for step in range(blocks - 1, 0, -1):
        held[step] = swapped(keys_values, "seq", step * GROUP)
    held = [held[step] for step in range(blocks)]
    level = jnp.minimum(mine, TOPK - 1)
    first = lax.cond(
        level == 0,
        lambda: first_block(queries, keys_values),
        lambda: jnp.zeros_like(queries),
    )
    branches = [functools.partial(later_block, columns) for columns in range(2, TOPK + 1)]
    return lax.switch(level, [lambda *_: first] + branches, queries, selected, held)


def solution(mesh):
    in_specs = (P("seq", "head"), P(("seq", "head"), None), P())
    out_specs = P("seq", "head")
    return jax.shard_map(shards, mesh=mesh, in_specs=in_specs, out_specs=out_specs, check_vma=False)
```

```python
import functools

import jax
import jax.numpy as jnp
from jax import lax
from jax.experimental import pallas as pl
from jax.experimental.pallas import tpu as pltpu
from jax.sharding import PartitionSpec as P

DH = 128
GROUP = 4
TOPK = 3
LOG2E = 1.4426950408889634
LOW = -3e38
VMEM = 16 << 20
LF, CF, ZF = 1, 0, ((1, 1), (0, 1), (1, 1))


def own(part, head):
    return 0, 0


def across(part, head):
    return 3, CF


def lane(part, head):
    return head ^ (((part ^ (part >> 1)) & 1) if LF else 0)


def beside(part, head):
    return 1 + lane(part, head), LF


def other_beside(part, head):
    return 2 - lane(part, head), LF


def swapped(rows, route):
    seq, head = lax.axis_size("seq"), lax.axis_size("head")
    routes = []
    for i in range(seq):
        for h in range(head):
            step, flip = route(i, h)
            routes.append((i * head + h, (i ^ step) * head + (h ^ flip)))
    return lax.ppermute(rows, ("seq", "head"), routes)


def earlier_block(step, place, head):
    lower = min(place, place ^ step * GROUP) // GROUP
    return step * GROUP, ZF[min(step, 3) - 1][lower & 1]


def other_core(part, head):
    return 0, 1


def kernel_call(body, out_shape, name, arrays):
    vmem = pl.BlockSpec(memory_space=pltpu.VMEM)
    return pl.pallas_call(
        body,
        out_shape=out_shape,
        in_specs=[vmem] * len(arrays),
        out_specs=jax.tree.map(lambda _: vmem, out_shape),
        compiler_params=pltpu.CompilerParams(vmem_limit_bytes=VMEM),
        name=name,
    )(*arrays)


def join_kernel(*refs):
    rows = refs[0].shape[0]
    for index, piece in enumerate(refs[:-1]):
        refs[-1][index * rows : (index + 1) * rows, :] = piece[...]


def join(pieces):
    rows, width = pieces[0].shape
    out = jax.ShapeDtypeStruct((len(pieces) * rows, width), pieces[0].dtype)
    return kernel_call(join_kernel, out, "join", pieces)


def pick_kernel(columns, blocks, selected_ref, *refs):
    held, messages = refs[:blocks], refs[blocks:]
    rows = held[0].shape[0]
    me = lax.axis_index("seq")
    mine = me // GROUP
    for index, route in enumerate((own, across, beside, other_beside)):
        step, _ = route(me % GROUP, lax.axis_index("head"))
        messages[index][0:rows, :] = held[0][...]
        for column in range(1, columns):
            picked = held[1][...]
            if columns > 2:
                wanted = selected_ref[pl.ds(me ^ step, 1), column : column + 1] ^ mine
                wanted = jnp.broadcast_to(wanted, picked.shape)
                for other in range(2, blocks):
                    picked = jnp.where(wanted == other, held[other][...], picked)
            messages[index][column * rows : (column + 1) * rows, :] = picked


def pick(columns, selected, held):
    rows, width = held[0].shape
    messages = [jax.ShapeDtypeStruct((columns * rows, width), held[0].dtype)] * GROUP
    body = functools.partial(pick_kernel, columns, len(held))
    return kernel_call(body, messages, f"pick_{columns}", [selected, *held])


def attend_kernel(rows, places, resumed, last, queries_ref, *refs):
    pieces, rest = refs[: len(places)], refs[len(places) :]
    state, outs = (rest[:3], rest[3:]) if resumed else ((), rest)
    tokens, width = queries_ref.shape
    heads = width // DH
    part = lax.axis_index("seq") % GROUP
    head = lax.axis_index("head")
    queries = queries_ref[...]
    stacked = jnp.concatenate([queries[:, h * DH : (h + 1) * DH] for h in range(heads)], axis=0)
    parts = [piece[:rows, :] for piece in pieces]
    parts += [piece[rows:, :] for piece in pieces if piece.shape[0] > rows]
    kv = jnp.concatenate(parts, axis=0)
    scores = lax.dot_general(
        stacked, kv[:, :DH], (((1,), (1,)), ((), ())), preferred_element_type=jnp.float32
    ) * (DH ** (-0.5) * LOG2E)
    edge = min(-(-len(pieces) * rows // DH) * DH, kv.shape[0])
    lane = lax.broadcasted_iota(jnp.int32, (1, edge), 1)
    position = jnp.zeros_like(lane)
    for index, (route, relayed) in enumerate(places):
        step, flip = route(part, head ^ relayed)
        start = (part ^ step) * tokens + (head ^ relayed ^ flip) * rows - index * rows
        inside = (lane >= index * rows) & (lane < (index + 1) * rows)
        position = jnp.where(inside, start + lane, position)
    token = lax.broadcasted_iota(jnp.int32, (heads * tokens, 1), 0) % tokens
    own = jnp.where(position <= part * tokens + token, scores[:, :edge], LOW)
    scores = jnp.concatenate([own, scores[:, edge:]], axis=1) if edge < kv.shape[0] else own
    top = jnp.broadcast_to(jnp.max(scores, axis=1, keepdims=True), (heads * tokens, DH))
    if resumed:
        before = state[0][...]
        top = jnp.maximum(top, before)
    columns = [scores[:, start : start + DH] for start in range(0, scores.shape[1], DH)]
    weights = jnp.concatenate([jnp.exp2(c - top[:, : c.shape[1]]).astype(jnp.bfloat16) for c in columns], axis=1)
    values = jnp.concatenate([kv[:, DH:], jnp.ones_like(kv[:, DH:])], axis=1)
    sums = jnp.dot(weights, values, preferred_element_type=jnp.float32)
    out, total = sums[:, :DH], sums[:, DH:]
    if resumed:
        scale = jnp.exp2(before - top)
        total += scale * state[1][...]
        out += scale * state[2][...]
    if not last:
        outs[0][...] = top
        outs[1][...] = total
        outs[2][...] = out
        return
    out /= total
    for h in range(heads):
        outs[0][:, h * DH : (h + 1) * DH] = out[h * tokens : (h + 1) * tokens].astype(outs[0].dtype)


def attend(rows, queries, placed, state=(), last=True):
    tokens, width = queries.shape
    running = jax.ShapeDtypeStruct((tokens * width // DH, DH), jnp.float32)
    out = jax.ShapeDtypeStruct(queries.shape, queries.dtype) if last else [running] * 3
    places, pieces = zip(*placed)
    body = functools.partial(attend_kernel, rows, places, bool(state), last)
    return kernel_call(body, out, f"attend_{len(pieces)}", [queries, *pieces, *state])


def first_block(queries, rows):
    diagonal = swapped(rows, across)
    first = swapped(rows, beside)
    diagonal, again = lax.optimization_barrier((diagonal, rows))
    near = join([rows, first, swapped(again, other_beside), diagonal])
    far = swapped(near, other_core)
    length = rows.shape[0]
    placed = []
    for relayed, piece in enumerate((near, far)):
        for index, route in enumerate((own, beside, other_beside, across)):
            placed.append(((route, relayed), piece[index * length : (index + 1) * length]))
    return attend(length, queries, placed)


def later_block(columns, queries, selected, held):
    length = held[0].shape[0]
    messages = pick(columns, selected, held)
    near = [messages[0]] + [swapped(m, route) for m, route in zip(messages[1:], (across, beside, other_beside))]
    far = [swapped(piece, other_core) for piece in near]
    placed = [((own, 0), near[0]), ((own, 1), far[0]), ((across, 0), near[1]), ((across, 1), far[1]), ((beside, 0), near[2]), ((other_beside, 0), near[3])]
    state = attend(length, queries, placed, last=False)
    placed = [((beside, 1), far[2]), ((other_beside, 1), far[3])]
    return attend(length, queries, placed, state)


def shards(queries, keys_values, selected):
    blocks = lax.axis_size("seq") // GROUP
    mine = lax.axis_index("seq") // GROUP
    held = {0: keys_values}
    for step in range(blocks - 1, 0, -1):
        held[step] = swapped(keys_values, functools.partial(earlier_block, step))
    held = [held[step] for step in range(blocks)]
    held[2], held[1] = lax.optimization_barrier((held[2], held[1]))
    held[3], held[2] = lax.optimization_barrier((held[3], held[2]))
    level = jnp.minimum(mine, TOPK - 1)
    first = lax.cond(
        level == 0,
        lambda: first_block(queries, keys_values),
        lambda: jnp.zeros_like(queries),
    )
    branches = [functools.partial(later_block, columns) for columns in range(2, TOPK + 1)]
    return lax.switch(level, [lambda *_: first] + branches, queries, selected, held)


def solution(mesh):
    in_specs = (P("seq", "head"), P(("seq", "head"), None), P())
    out_specs = P("seq", "head")
    return jax.shard_map(shards, mesh=mesh, in_specs=in_specs, out_specs=out_specs, check_vma=False)
```

```python
import functools

import jax
import jax.numpy as jnp
from jax import lax
from jax.experimental import pallas as pl
from jax.experimental.pallas import tpu as pltpu
from jax.sharding import PartitionSpec as P

DH = 128
GROUP = 4
TOPK = 3
LOG2E = 1.4426950408889634
LOW = -3e38
VMEM = 16 << 20
CROSSES = ((1, 1, 1, 1), (0, 1, 0, 0), (1, 0, 0, 0))


def own(place, head):
    return 0, 0


def across(place, head):
    return 3, place // GROUP & 1


def lane(place, head):
    return head ^ ((place ^ place >> 1) & 1)


def beside(place, head):
    return 1 + lane(place, head), 1


def other_beside(place, head):
    return 2 - lane(place, head), 1


def other_core(place, head):
    return 0, 1


def block_away(step, place, head):
    lower = min(place, place ^ step * GROUP) // GROUP
    return step * GROUP, CROSSES[min(step, 3) - 1][lower & 3]


def swapped(rows, route):
    seq, head = lax.axis_size("seq"), lax.axis_size("head")
    pairs = []
    for i in range(seq):
        for h in range(head):
            step, flip = route(i, h)
            pairs.append((i * head + h, (i ^ step) * head + (h ^ flip)))
    return lax.ppermute(rows, ("seq", "head"), pairs)


def kernel_call(body, out_shape, name, arrays):
    vmem = pl.BlockSpec(memory_space=pltpu.VMEM)
    return pl.pallas_call(
        body,
        out_shape=out_shape,
        in_specs=[vmem] * len(arrays),
        out_specs=jax.tree.map(lambda _: vmem, out_shape),
        compiler_params=pltpu.CompilerParams(vmem_limit_bytes=VMEM),
        name=name,
    )(*arrays)


def join_kernel(*refs):
    rows = refs[0].shape[0]
    for index, piece in enumerate(refs[:-1]):
        refs[-1][index * rows : (index + 1) * rows, :] = piece[...]


def join(pieces):
    rows, width = pieces[0].shape
    out = jax.ShapeDtypeStruct((len(pieces) * rows, width), pieces[0].dtype)
    return kernel_call(join_kernel, out, "join", pieces)


def pick_kernel(columns, blocks, selected_ref, *refs):
    held, messages = refs[:blocks], refs[blocks:]
    rows = held[0].shape[0]
    me = lax.axis_index("seq")
    mine = me // GROUP
    for index, route in enumerate((own, across, beside, other_beside)):
        step, _ = route(me, lax.axis_index("head"))
        messages[index][0:rows, :] = held[0][...]
        for column in range(1, columns):
            picked = held[1][...]
            if columns > 2:
                wanted = selected_ref[pl.ds(me ^ step, 1), column : column + 1] ^ mine
                wanted = jnp.broadcast_to(wanted, picked.shape)
                for other in range(2, blocks):
                    picked = jnp.where(wanted == other, held[other][...], picked)
            messages[index][column * rows : (column + 1) * rows, :] = picked


def pick(columns, selected, held):
    rows, width = held[0].shape
    messages = [jax.ShapeDtypeStruct((columns * rows, width), held[0].dtype)] * GROUP
    body = functools.partial(pick_kernel, columns, len(held))
    return kernel_call(body, messages, f"pick_{columns}", [selected, *held])


def attend_kernel(rows, places, resumed, last, queries_ref, *refs):
    pieces, rest = refs[: len(places)], refs[len(places) :]
    state, outs = (rest[:3], rest[3:]) if resumed else ((), rest)
    tokens, width = queries_ref.shape
    heads = width // DH
    me = lax.axis_index("seq")
    head = lax.axis_index("head")
    queries = queries_ref[...]
    stacked = jnp.concatenate([queries[:, h * DH : (h + 1) * DH] for h in range(heads)], axis=0)
    parts = [piece[:rows, :] for piece in pieces]
    parts += [piece[rows:, :] for piece in pieces if piece.shape[0] > rows]
    kv = jnp.concatenate(parts, axis=0)
    scores = lax.dot_general(
        stacked, kv[:, :DH], (((1,), (1,)), ((), ())), preferred_element_type=jnp.float32
    ) * (DH ** (-0.5) * LOG2E)
    edge = min(-(-len(pieces) * rows // DH) * DH, kv.shape[0])
    lane = lax.broadcasted_iota(jnp.int32, (1, edge), 1)
    position = jnp.zeros_like(lane)
    for index, (route, relayed) in enumerate(places):
        step, flip = route(me, head ^ relayed)
        start = ((me ^ step) % GROUP) * tokens + (head ^ relayed ^ flip) * rows - index * rows
        inside = (lane >= index * rows) & (lane < (index + 1) * rows)
        position = jnp.where(inside, start + lane, position)
    token = lax.broadcasted_iota(jnp.int32, (heads * tokens, 1), 0) % tokens
    own = jnp.where(position <= (me % GROUP) * tokens + token, scores[:, :edge], LOW)
    scores = jnp.concatenate([own, scores[:, edge:]], axis=1) if edge < kv.shape[0] else own
    top = jnp.broadcast_to(jnp.max(scores, axis=1, keepdims=True), (heads * tokens, DH))
    if resumed:
        before = state[0][...]
        top = jnp.maximum(top, before)
    columns = [scores[:, start : start + DH] for start in range(0, scores.shape[1], DH)]
    weights = jnp.concatenate([jnp.exp2(c - top[:, : c.shape[1]]).astype(jnp.bfloat16) for c in columns], axis=1)
    values = jnp.concatenate([kv[:, DH:], jnp.ones_like(kv[:, DH:])], axis=1)
    sums = jnp.dot(weights, values, preferred_element_type=jnp.float32)
    out, total = sums[:, :DH], sums[:, DH:]
    if resumed:
        scale = jnp.exp2(before - top)
        total += scale * state[1][...]
        out += scale * state[2][...]
    if not last:
        outs[0][...] = top
        outs[1][...] = total
        outs[2][...] = out
        return
    out /= total
    for h in range(heads):
        outs[0][:, h * DH : (h + 1) * DH] = out[h * tokens : (h + 1) * tokens].astype(outs[0].dtype)


def attend(rows, queries, placed, state=(), last=True):
    tokens, width = queries.shape
    running = jax.ShapeDtypeStruct((tokens * width // DH, DH), jnp.float32)
    out = jax.ShapeDtypeStruct(queries.shape, queries.dtype) if last else [running] * 3
    places, pieces = zip(*placed)
    body = functools.partial(attend_kernel, rows, places, bool(state), last)
    return kernel_call(body, out, f"attend_{len(pieces)}", [queries, *pieces, *state])


def first_block(queries, rows):
    diagonal = swapped(rows, across)
    first = swapped(rows, beside)
    diagonal, again = lax.optimization_barrier((diagonal, rows))
    near = join([rows, first, swapped(again, other_beside), diagonal])
    far = swapped(near, other_core)
    length = rows.shape[0]
    placed = []
    for relayed, piece in enumerate((near, far)):
        for index, route in enumerate((own, beside, other_beside, across)):
            placed.append(((route, relayed), piece[index * length : (index + 1) * length]))
    return attend(length, queries, placed)


def later_block(columns, queries, selected, held):
    length = held[0].shape[0]
    messages = pick(columns, selected, held)
    near = [messages[0]] + [swapped(m, route) for m, route in zip(messages[1:], (across, beside, other_beside))]
    far = [swapped(piece, other_core) for piece in near]
    placed = [((own, 0), near[0]), ((own, 1), far[0]), ((across, 0), near[1]), ((across, 1), far[1]), ((beside, 0), near[2]), ((other_beside, 0), near[3])]
    state = attend(length, queries, placed, last=False)
    placed = [((beside, 1), far[2]), ((other_beside, 1), far[3])]
    return attend(length, queries, placed, state)


def shards(queries, keys_values, selected):
    blocks = lax.axis_size("seq") // GROUP
    mine = lax.axis_index("seq") // GROUP
    held = {0: keys_values}
    for step in range(blocks - 1, 0, -1):
        held[step] = swapped(keys_values, functools.partial(block_away, step))
    held = [held[step] for step in range(blocks)]
    held[2], held[1] = lax.optimization_barrier((held[2], held[1]))
    held[3], held[2] = lax.optimization_barrier((held[3], held[2]))
    level = jnp.minimum(mine, TOPK - 1)
    first = lax.cond(
        level == 0,
        lambda: first_block(queries, keys_values),
        lambda: jnp.zeros_like(queries),
    )
    branches = [functools.partial(later_block, columns) for columns in range(2, TOPK + 1)]
    return lax.switch(level, [lambda *_: first] + branches, queries, selected, held)


def solution(mesh):
    in_specs = (P("seq", "head"), P(("seq", "head"), None), P())
    out_specs = P("seq", "head")
    return jax.shard_map(shards, mesh=mesh, in_specs=in_specs, out_specs=out_specs, check_vma=False)
```

```python
import functools

import jax
import jax.numpy as jnp
from jax import lax
from jax.experimental import pallas as pl
from jax.experimental.pallas import tpu as pltpu
from jax.sharding import PartitionSpec as P

DH = 128
GROUP = 4
TOPK = 3
LOG2E = 1.4426950408889634
LOW = -3e38
VMEM = 16 << 20
CROSSES = ((1, 1, 1, 1), (0, 1, 0, 0), (1, 0, 0, 0))


def own(place, head):
    return 0, 0


def across(place, head):
    return 3, place // GROUP & 1


def lane(place, head):
    return head ^ ((place ^ place >> 1) & 1)


def beside(place, head):
    return 1 + lane(place, head), 1


def other_beside(place, head):
    return 2 - lane(place, head), 1


def other_core(place, head):
    return 0, 1


def block_away(step, place, head):
    lower = min(place, place ^ step * GROUP) // GROUP
    return step * GROUP, CROSSES[min(step, 3) - 1][lower & 3]


def swapped(rows, route):
    seq, head = lax.axis_size("seq"), lax.axis_size("head")
    pairs = []
    for i in range(seq):
        for h in range(head):
            step, flip = route(i, h)
            pairs.append((i * head + h, (i ^ step) * head + (h ^ flip)))
    return lax.ppermute(rows, ("seq", "head"), pairs)


def kernel_call(body, out_shape, name, arrays):
    vmem = pl.BlockSpec(memory_space=pltpu.VMEM)
    return pl.pallas_call(
        body,
        out_shape=out_shape,
        in_specs=[vmem] * len(arrays),
        out_specs=jax.tree.map(lambda _: vmem, out_shape),
        compiler_params=pltpu.CompilerParams(vmem_limit_bytes=VMEM),
        name=name,
    )(*arrays)


def join_kernel(*refs):
    rows = refs[0].shape[0]
    for index, piece in enumerate(refs[:-1]):
        refs[-1][index * rows : (index + 1) * rows, :] = piece[...]


def join(pieces):
    rows, width = pieces[0].shape
    out = jax.ShapeDtypeStruct((len(pieces) * rows, width), pieces[0].dtype)
    return kernel_call(join_kernel, out, "join", pieces)


def plan_kernel(selected_ref, wanted_ref):
    me = lax.axis_index("seq")
    for index, route in enumerate((own, across, beside, other_beside)):
        step, _ = route(me, lax.axis_index("head"))
        for column in range(1, TOPK):
            wanted = selected_ref[pl.ds(me ^ step, 1), column : column + 1] ^ (me // GROUP)
            row = index * (TOPK - 1) + column - 1
            wanted_ref[row : row + 1, :] = jnp.broadcast_to(wanted, (1, DH))


def pick_kernel(columns, blocks, wanted_ref, *refs):
    held, messages = refs[:blocks], refs[blocks:]
    rows = held[0].shape[0]
    for index in range(GROUP):
        messages[index][0:rows, :] = held[0][...]
        for column in range(1, columns):
            picked = held[1][...]
            if columns > 2:
                row = index * (TOPK - 1) + column - 1
                wanted = jnp.broadcast_to(wanted_ref[row : row + 1, :], (rows, DH))
                wanted = jnp.concatenate([wanted, wanted], axis=1)
                for other in range(2, blocks):
                    picked = jnp.where(wanted == other, held[other][...], picked)
            messages[index][column * rows : (column + 1) * rows, :] = picked


def pick(columns, selected, held):
    rows, width = held[0].shape
    messages = [jax.ShapeDtypeStruct((columns * rows, width), held[0].dtype)] * GROUP
    body = functools.partial(pick_kernel, columns, len(held))
    return kernel_call(body, messages, f"pick_{columns}", [selected, *held])


def attend_kernel(rows, places, resumed, last, queries_ref, *refs):
    pieces, rest = refs[: len(places)], refs[len(places) :]
    state, outs = (rest[:3], rest[3:]) if resumed else ((), rest)
    tokens, width = queries_ref.shape
    heads = width // DH
    me = lax.axis_index("seq")
    head = lax.axis_index("head")
    queries = queries_ref[...]
    stacked = jnp.concatenate([queries[:, h * DH : (h + 1) * DH] for h in range(heads)], axis=0)
    parts = [piece[:rows, :] for piece in pieces]
    parts += [piece[rows:, :] for piece in pieces if piece.shape[0] > rows]
    kv = jnp.concatenate(parts, axis=0)
    scores = lax.dot_general(
        stacked, kv[:, :DH], (((1,), (1,)), ((), ())), preferred_element_type=jnp.float32
    ) * (DH ** (-0.5) * LOG2E)
    edge = min(-(-len(pieces) * rows // DH) * DH, kv.shape[0])
    lane = lax.broadcasted_iota(jnp.int32, (1, edge), 1)
    position = jnp.zeros_like(lane)
    for index, (route, relayed) in enumerate(places):
        step, flip = route(me, head ^ relayed)
        start = ((me ^ step) % GROUP) * tokens + (head ^ relayed ^ flip) * rows - index * rows
        inside = (lane >= index * rows) & (lane < (index + 1) * rows)
        position = jnp.where(inside, start + lane, position)
    token = lax.broadcasted_iota(jnp.int32, (heads * tokens, 1), 0) % tokens
    own = jnp.where(position <= (me % GROUP) * tokens + token, scores[:, :edge], LOW)
    scores = jnp.concatenate([own, scores[:, edge:]], axis=1) if edge < kv.shape[0] else own
    top = jnp.broadcast_to(jnp.max(scores, axis=1, keepdims=True), (heads * tokens, DH))
    if resumed:
        before = state[0][...]
        top = jnp.maximum(top, before)
    columns = [scores[:, start : start + DH] for start in range(0, scores.shape[1], DH)]
    weights = jnp.concatenate([jnp.exp2(c - top[:, : c.shape[1]]).astype(jnp.bfloat16) for c in columns], axis=1)
    values = jnp.concatenate([kv[:, DH:], jnp.ones_like(kv[:, DH:])], axis=1)
    sums = jnp.dot(weights, values, preferred_element_type=jnp.float32)
    out, total = sums[:, :DH], sums[:, DH:]
    if resumed:
        scale = jnp.exp2(before - top)
        total += scale * state[1][...]
        out += scale * state[2][...]
    if not last:
        outs[0][...] = top
        outs[1][...] = total
        outs[2][...] = out
        return
    out /= total
    for h in range(heads):
        outs[0][:, h * DH : (h + 1) * DH] = out[h * tokens : (h + 1) * tokens].astype(outs[0].dtype)


def attend(rows, queries, placed, state=(), last=True):
    tokens, width = queries.shape
    running = jax.ShapeDtypeStruct((tokens * width // DH, DH), jnp.float32)
    out = jax.ShapeDtypeStruct(queries.shape, queries.dtype) if last else [running] * 3
    places, pieces = zip(*placed)
    body = functools.partial(attend_kernel, rows, places, bool(state), last)
    return kernel_call(body, out, f"attend_{len(pieces)}", [queries, *pieces, *state])


def first_block(queries, rows):
    diagonal = swapped(rows, across)
    first = swapped(rows, beside)
    diagonal, again = lax.optimization_barrier((diagonal, rows))
    near = join([rows, first, swapped(again, other_beside), diagonal])
    far = swapped(near, other_core)
    length = rows.shape[0]
    placed = []
    for relayed, piece in enumerate((near, far)):
        for index, route in enumerate((own, beside, other_beside, across)):
            placed.append(((route, relayed), piece[index * length : (index + 1) * length]))
    return attend(length, queries, placed)


def later_block(columns, queries, selected, held):
    length = held[0].shape[0]
    messages = pick(columns, selected, held)
    near = [messages[0]] + [swapped(m, route) for m, route in zip(messages[1:], (across, beside, other_beside))]
    far = [swapped(piece, other_core) for piece in near]
    placed = [((own, 0), near[0]), ((own, 1), far[0]), ((across, 0), near[1]), ((across, 1), far[1]), ((beside, 0), near[2]), ((other_beside, 0), near[3])]
    state = attend(length, queries, placed, last=False)
    placed = [((beside, 1), far[2]), ((other_beside, 1), far[3])]
    return attend(length, queries, placed, state)


def shards(queries, keys_values, selected):
    blocks = lax.axis_size("seq") // GROUP
    mine = lax.axis_index("seq") // GROUP
    held = {0: keys_values}
    for step in range(blocks - 1, 0, -1):
        held[step] = swapped(keys_values, functools.partial(block_away, step))
    held = [held[step] for step in range(blocks)]
    held[2], held[1] = lax.optimization_barrier((held[2], held[1]))
    held[3], held[2] = lax.optimization_barrier((held[3], held[2]))
    selected = kernel_call(plan_kernel, jax.ShapeDtypeStruct((2 * GROUP, DH), jnp.int32), "plan", [selected])
    level = jnp.minimum(mine, TOPK - 1)
    first = lax.cond(
        level == 0,
        lambda: first_block(queries, keys_values),
        lambda: jnp.zeros_like(queries),
    )
    branches = [functools.partial(later_block, columns) for columns in range(2, TOPK + 1)]
    return lax.switch(level, [lambda *_: first] + branches, queries, selected, held)


def solution(mesh):
    in_specs = (P("seq", "head"), P(("seq", "head"), None), P())
    out_specs = P("seq", "head")
    return jax.shard_map(shards, mesh=mesh, in_specs=in_specs, out_specs=out_specs, check_vma=False)
```

```python
import functools

import jax
import jax.numpy as jnp
from jax import lax
from jax.experimental import pallas as pl
from jax.experimental.pallas import tpu as pltpu
from jax.sharding import PartitionSpec as P

DH = 128
GROUP = 4
TOPK = 3
LOG2E = 1.4426950408889634
LOW = -3e38
SCALE = DH ** (-0.5) * LOG2E
VMEM = 16 << 20
CROSSES = ((1, 1, 1, 1), (0, 1, 0, 0), (1, 0, 0, 0))


def own(place, head):
    return 0, 0


def across(place, head):
    return 3, place // GROUP & 1


def lane(place, head):
    return head ^ ((place ^ place >> 1) & 1)


def beside(place, head):
    return 1 + lane(place, head), 1


def other_beside(place, head):
    return 2 - lane(place, head), 1


def other_core(place, head):
    return 0, 1


def block_away(step, place, head):
    lower = min(place, place ^ step * GROUP) // GROUP
    return step * GROUP, CROSSES[min(step, 3) - 1][lower & 3]


def swapped(rows, route):
    seq, head = lax.axis_size("seq"), lax.axis_size("head")
    pairs = []
    for i in range(seq):
        for h in range(head):
            step, flip = route(i, h)
            pairs.append((i * head + h, (i ^ step) * head + (h ^ flip)))
    return lax.ppermute(rows, ("seq", "head"), pairs)


def kernel_call(body, out_shape, name, arrays):
    vmem = pl.BlockSpec(memory_space=pltpu.VMEM)
    return pl.pallas_call(
        body,
        out_shape=out_shape,
        in_specs=[vmem] * len(arrays),
        out_specs=jax.tree.map(lambda _: vmem, out_shape),
        compiler_params=pltpu.CompilerParams(vmem_limit_bytes=VMEM),
        name=name,
    )(*arrays)


def join_kernel(*refs):
    rows = refs[0].shape[0]
    for index, piece in enumerate(refs[:-1]):
        refs[-1][index * rows : (index + 1) * rows, :] = piece[...]


def join(pieces):
    rows, width = pieces[0].shape
    out = jax.ShapeDtypeStruct((len(pieces) * rows, width), pieces[0].dtype)
    return kernel_call(join_kernel, out, "join", pieces)


def plan_kernel(selected_ref, wanted_ref):
    me = lax.axis_index("seq")
    for index, route in enumerate((own, across, beside, other_beside)):
        step, _ = route(me, lax.axis_index("head"))
        for column in range(1, TOPK):
            wanted = selected_ref[pl.ds(me ^ step, 1), column : column + 1] ^ (me // GROUP)
            row = index * (TOPK - 1) + column - 1
            wanted_ref[row : row + 1, :] = jnp.broadcast_to(wanted, (1, DH))


def pick_kernel(columns, blocks, wanted_ref, *refs):
    held, messages = refs[:blocks], refs[blocks:]
    rows = held[0].shape[0]
    for index in range(GROUP):
        messages[index][0:rows, :] = held[0][...]
        for column in range(1, columns):
            picked = held[1][...]
            if columns > 2:
                row = index * (TOPK - 1) + column - 1
                wanted = jnp.broadcast_to(wanted_ref[row : row + 1, :], (rows, DH))
                wanted = jnp.concatenate([wanted, wanted], axis=1)
                for other in range(2, blocks):
                    picked = jnp.where(wanted == other, held[other][...], picked)
            messages[index][column * rows : (column + 1) * rows, :] = picked


def pick(columns, selected, held):
    rows, width = held[0].shape
    messages = [jax.ShapeDtypeStruct((columns * rows, width), held[0].dtype)] * GROUP
    body = functools.partial(pick_kernel, columns, len(held))
    return kernel_call(body, messages, f"pick_{columns}", [selected, *held])


def attend_kernel(rows, places, resumed, last, queries_ref, *refs):
    pieces, rest = refs[: len(places)], refs[len(places) :]
    state, outs = (rest[:3], rest[3:]) if resumed else ((), rest)
    tokens, width = queries_ref.shape
    heads = width // DH
    me = lax.axis_index("seq")
    head = lax.axis_index("head")
    queries = queries_ref[...]
    stacked = jnp.concatenate([queries[:, h * DH : (h + 1) * DH] for h in range(heads)], axis=0)
    parts = [piece[:rows, :] for piece in pieces]
    parts += [piece[rows:, :] for piece in pieces if piece.shape[0] > rows]
    kv = jnp.concatenate(parts, axis=0)
    scores = lax.dot_general(
        stacked, kv[:, :DH], (((1,), (1,)), ((), ())), preferred_element_type=jnp.float32
    )
    edge = min(-(-len(pieces) * rows // DH) * DH, kv.shape[0])
    lane = lax.broadcasted_iota(jnp.int32, (1, edge), 1)
    position = jnp.zeros_like(lane)
    for index, (route, relayed) in enumerate(places):
        step, flip = route(me, head ^ relayed)
        start = ((me ^ step) % GROUP) * tokens + (head ^ relayed ^ flip) * rows - index * rows
        inside = (lane >= index * rows) & (lane < (index + 1) * rows)
        position = jnp.where(inside, start + lane, position)
    token = lax.broadcasted_iota(jnp.int32, (heads * tokens, 1), 0) % tokens
    own = jnp.where(position <= (me % GROUP) * tokens + token, scores[:, :edge], LOW)
    scores = jnp.concatenate([own, scores[:, edge:]], axis=1) if edge < kv.shape[0] else own
    top = jnp.broadcast_to(jnp.max(scores, axis=1, keepdims=True), (heads * tokens, DH))
    if resumed:
        before = state[0][...]
        top = jnp.maximum(top, before)
    columns = [scores[:, start : start + DH] for start in range(0, scores.shape[1], DH)]
    weights = jnp.concatenate([jnp.exp2((c - top[:, : c.shape[1]]) * SCALE).astype(jnp.bfloat16) for c in columns], axis=1)
    values = jnp.concatenate([kv[:, DH:], jnp.ones_like(kv[:, DH:])], axis=1)
    sums = jnp.dot(weights, values, preferred_element_type=jnp.float32)
    out, total = sums[:, :DH], sums[:, DH:]
    if resumed:
        scale = jnp.exp2((before - top) * SCALE)
        total += scale * state[1][...]
        out += scale * state[2][...]
    if not last:
        outs[0][...] = top
        outs[1][...] = total
        outs[2][...] = out
        return
    out /= total
    for h in range(heads):
        outs[0][:, h * DH : (h + 1) * DH] = out[h * tokens : (h + 1) * tokens].astype(outs[0].dtype)


def attend(rows, queries, placed, state=(), last=True):
    tokens, width = queries.shape
    running = jax.ShapeDtypeStruct((tokens * width // DH, DH), jnp.float32)
    out = jax.ShapeDtypeStruct(queries.shape, queries.dtype) if last else [running] * 3
    places, pieces = zip(*placed)
    body = functools.partial(attend_kernel, rows, places, bool(state), last)
    return kernel_call(body, out, f"attend_{len(pieces)}", [queries, *pieces, *state])


def first_block(queries, rows):
    diagonal = swapped(rows, across)
    first = swapped(rows, beside)
    diagonal, again = lax.optimization_barrier((diagonal, rows))
    near = join([rows, first, swapped(again, other_beside), diagonal])
    far = swapped(near, other_core)
    length = rows.shape[0]
    placed = []
    for relayed, piece in enumerate((near, far)):
        for index, route in enumerate((own, beside, other_beside, across)):
            placed.append(((route, relayed), piece[index * length : (index + 1) * length]))
    return attend(length, queries, placed)


def later_block(columns, queries, selected, held):
    length = held[0].shape[0]
    messages = pick(columns, selected, held)
    near = [messages[0]] + [swapped(m, route) for m, route in zip(messages[1:], (across, beside, other_beside))]
    state = attend(length, queries, [((own, 0), near[0]), ((across, 0), near[1])], last=False)
    near[3], *state = lax.optimization_barrier((near[3], *state))
    far = [swapped(piece, other_core) for piece in near]
    placed = [((own, 1), far[0]), ((across, 1), far[1]), ((beside, 0), near[2]), ((other_beside, 0), near[3])]
    state = attend(length, queries, placed, state, last=False)
    placed = [((beside, 1), far[2]), ((other_beside, 1), far[3])]
    return attend(length, queries, placed, state)


def shards(queries, keys_values, selected):
    blocks = lax.axis_size("seq") // GROUP
    mine = lax.axis_index("seq") // GROUP
    held = {0: keys_values}
    for step in range(blocks - 1, 0, -1):
        held[step] = swapped(keys_values, functools.partial(block_away, step))
    held = [held[step] for step in range(blocks)]
    held[2], held[1] = lax.optimization_barrier((held[2], held[1]))
    held[3], held[2] = lax.optimization_barrier((held[3], held[2]))
    selected = kernel_call(plan_kernel, jax.ShapeDtypeStruct((2 * GROUP, DH), jnp.int32), "plan", [selected])
    level = jnp.minimum(mine, TOPK - 1)
    first = lax.cond(
        level == 0,
        lambda: first_block(queries, keys_values),
        lambda: jnp.zeros_like(queries),
    )
    branches = [functools.partial(later_block, columns) for columns in range(2, TOPK + 1)]
    return lax.switch(level, [lambda *_: first] + branches, queries, selected, held)


def solution(mesh):
    in_specs = (P("seq", "head"), P(("seq", "head"), None), P())
    out_specs = P("seq", "head")
    return jax.shard_map(shards, mesh=mesh, in_specs=in_specs, out_specs=out_specs, check_vma=False)
```

```python
import functools

import jax
import jax.numpy as jnp
from jax import lax
from jax.experimental import pallas as pl
from jax.experimental.pallas import tpu as pltpu
from jax.sharding import PartitionSpec as P

DH = 128
GROUP = 4
TOPK = 3
LOG2E = 1.4426950408889634
LOW = -3e38
SCALE = DH ** (-0.5) * LOG2E
VMEM = 16 << 20
CROSSES = ((1, 1, 1, 1), (0, 1, 0, 0), (1, 0, 0, 0))


def own(place, head):
    return 0, 0


def across(place, head):
    return 3, place // GROUP & 1


def lane(place, head):
    return head ^ ((place ^ place >> 1) & 1)


def beside(place, head):
    return 1 + lane(place, head), 1


def other_beside(place, head):
    return 2 - lane(place, head), 1


def other_core(place, head):
    return 0, 1


def block_away(step, place, head):
    lower = min(place, place ^ step * GROUP) // GROUP
    return step * GROUP, CROSSES[min(step, 3) - 1][lower & 3]


def swapped(rows, route):
    seq, head = lax.axis_size("seq"), lax.axis_size("head")
    pairs = []
    for i in range(seq):
        for h in range(head):
            step, flip = route(i, h)
            pairs.append((i * head + h, (i ^ step) * head + (h ^ flip)))
    return lax.ppermute(rows, ("seq", "head"), pairs)


def kernel_call(body, out_shape, name, arrays):
    vmem = pl.BlockSpec(memory_space=pltpu.VMEM)
    return pl.pallas_call(
        body,
        out_shape=out_shape,
        in_specs=[vmem] * len(arrays),
        out_specs=jax.tree.map(lambda _: vmem, out_shape),
        compiler_params=pltpu.CompilerParams(vmem_limit_bytes=VMEM),
        name=name,
    )(*arrays)


def join_kernel(*refs):
    rows = refs[0].shape[0]
    for index, piece in enumerate(refs[:-1]):
        refs[-1][index * rows : (index + 1) * rows, :] = piece[...]


def join(pieces):
    rows, width = pieces[0].shape
    out = jax.ShapeDtypeStruct((len(pieces) * rows, width), pieces[0].dtype)
    return kernel_call(join_kernel, out, "join", pieces)


def plan_kernel(selected_ref, wanted_ref):
    me = lax.axis_index("seq")
    for index, route in enumerate((own, across, beside, other_beside)):
        step, _ = route(me, lax.axis_index("head"))
        for column in range(1, TOPK):
            wanted = selected_ref[pl.ds(me ^ step, 1), column : column + 1] ^ (me // GROUP)
            row = index * (TOPK - 1) + column - 1
            wanted_ref[row : row + 1, :] = jnp.broadcast_to(wanted, (1, DH))


def pick_kernel(columns, blocks, wanted_ref, *refs):
    held, messages = refs[:blocks], refs[blocks:]
    rows = held[0].shape[0]
    for index in range(GROUP):
        messages[index][0:rows, :] = held[0][...]
        for column in range(1, columns):
            picked = held[1][...]
            if columns > 2:
                row = index * (TOPK - 1) + column - 1
                wanted = jnp.broadcast_to(wanted_ref[row : row + 1, :], (rows, DH))
                wanted = jnp.concatenate([wanted, wanted], axis=1)
                for other in range(2, blocks):
                    picked = jnp.where(wanted == other, held[other][...], picked)
            messages[index][column * rows : (column + 1) * rows, :] = picked


def pick(columns, selected, held):
    rows, width = held[0].shape
    messages = [jax.ShapeDtypeStruct((columns * rows, width), held[0].dtype)] * GROUP
    body = functools.partial(pick_kernel, columns, len(held))
    return kernel_call(body, messages, f"pick_{columns}", [selected, *held])


def attend_kernel(rows, places, resumed, last, queries_ref, *refs):
    pieces, rest = refs[: len(places)], refs[len(places) :]
    state, outs = (rest[:3], rest[3:]) if resumed else ((), rest)
    tokens, width = queries_ref.shape
    heads = width // DH
    me = lax.axis_index("seq")
    head = lax.axis_index("head")
    queries = queries_ref[...]
    stacked = jnp.concatenate([queries[:, h * DH : (h + 1) * DH] for h in range(heads)], axis=0)
    parts = [piece[:rows, :] for piece in pieces]
    parts += [piece[rows:, :] for piece in pieces if piece.shape[0] > rows]
    kv = jnp.concatenate(parts, axis=0)
    scores = lax.dot_general(
        stacked, kv[:, :DH], (((1,), (1,)), ((), ())), preferred_element_type=jnp.float32
    )
    edge = min(-(-len(pieces) * rows // DH) * DH, kv.shape[0])
    lane = lax.broadcasted_iota(jnp.int32, (1, edge), 1)
    position = jnp.zeros_like(lane)
    for index, (route, relayed) in enumerate(places):
        step, flip = route(me, head ^ relayed)
        start = ((me ^ step) % GROUP) * tokens + (head ^ relayed ^ flip) * rows - index * rows
        inside = (lane >= index * rows) & (lane < (index + 1) * rows)
        position = jnp.where(inside, start + lane, position)
    token = lax.broadcasted_iota(jnp.int32, (heads * tokens, 1), 0) % tokens
    own = jnp.where(position <= (me % GROUP) * tokens + token, scores[:, :edge], LOW)
    scores = jnp.concatenate([own, scores[:, edge:]], axis=1) if edge < kv.shape[0] else own
    top = jnp.broadcast_to(jnp.max(scores, axis=1, keepdims=True), (heads * tokens, DH))
    if resumed:
        before = state[0][...]
        top = jnp.maximum(top, before)
    columns = [scores[:, start : start + DH] for start in range(0, scores.shape[1], DH)]
    weights = jnp.concatenate([jnp.exp2((c - top[:, : c.shape[1]]) * SCALE).astype(jnp.bfloat16) for c in columns], axis=1)
    values = jnp.concatenate([kv[:, DH:], jnp.ones_like(kv[:, DH:])], axis=1)
    sums = jnp.dot(weights, values, preferred_element_type=jnp.float32)
    out, total = sums[:, :DH], sums[:, DH:]
    if resumed:
        scale = jnp.exp2((before - top) * SCALE)
        total += scale * state[1][...]
        out += scale * state[2][...]
    if not last:
        outs[0][...] = top
        outs[1][...] = total
        outs[2][...] = out
        return
    out /= total
    for h in range(heads):
        outs[0][:, h * DH : (h + 1) * DH] = out[h * tokens : (h + 1) * tokens].astype(outs[0].dtype)


def attend(rows, queries, placed, state=(), last=True):
    tokens, width = queries.shape
    running = jax.ShapeDtypeStruct((tokens * width // DH, DH), jnp.float32)
    out = jax.ShapeDtypeStruct(queries.shape, queries.dtype) if last else [running] * 3
    places, pieces = zip(*placed)
    body = functools.partial(attend_kernel, rows, places, bool(state), last)
    return kernel_call(body, out, f"attend_{len(pieces)}", [queries, *pieces, *state])


def first_block(queries, rows):
    diagonal = swapped(rows, across)
    first = swapped(rows, beside)
    diagonal, again = lax.optimization_barrier((diagonal, rows))
    near = join([rows, first, swapped(again, other_beside), diagonal])
    far = swapped(near, other_core)
    length = rows.shape[0]
    placed = []
    for relayed, piece in enumerate((near, far)):
        for index, route in enumerate((own, beside, other_beside, across)):
            placed.append(((route, relayed), piece[index * length : (index + 1) * length]))
    return attend(length, queries, placed)


def later_block(columns, queries, selected, held):
    length = held[0].shape[0]
    messages = pick(columns, selected, held)
    near = [messages[0]] + [swapped(m, route) for m, route in zip(messages[1:], (across, beside, other_beside))]
    state = attend(length, queries, [((own, 0), near[0]), ((across, 0), near[1])], last=False)
    near[3], *state = lax.optimization_barrier((near[3], *state))
    far = [swapped(piece, other_core) for piece in near]
    placed = [((own, 1), far[0]), ((across, 1), far[1]), ((beside, 0), near[2]), ((other_beside, 0), near[3])]
    state = attend(length, queries, placed, state, last=False)
    placed = [((beside, 1), far[2]), ((other_beside, 1), far[3])]
    return attend(length, queries, placed, state)


def shards(queries, keys_values, selected):
    blocks = lax.axis_size("seq") // GROUP
    mine = lax.axis_index("seq") // GROUP
    held = {0: keys_values}
    for step in range(blocks - 1, 0, -1):
        held[step] = swapped(keys_values, functools.partial(block_away, step))
    held = [held[step] for step in range(blocks)]
    held[2], held[1] = lax.optimization_barrier((held[2], held[1]))
    held[3], held[2] = lax.optimization_barrier((held[3], held[2]))
    selected, held[1] = lax.optimization_barrier((selected, held[1]))
    selected = kernel_call(plan_kernel, jax.ShapeDtypeStruct((2 * GROUP, DH), jnp.int32), "plan", [selected])
    level = jnp.minimum(mine, TOPK - 1)
    first = lax.cond(
        level == 0,
        lambda: first_block(queries, keys_values),
        lambda: jnp.zeros_like(queries),
    )
    branches = [functools.partial(later_block, columns) for columns in range(2, TOPK + 1)]
    return lax.switch(level, [lambda *_: first] + branches, queries, selected, held)


def solution(mesh):
    in_specs = (P("seq", "head"), P(("seq", "head"), None), P())
    out_specs = P("seq", "head")
    return jax.shard_map(shards, mesh=mesh, in_specs=in_specs, out_specs=out_specs, check_vma=False)
```

```python
import functools

import jax
import jax.numpy as jnp
from jax import lax
from jax.experimental import pallas as pl
from jax.experimental.pallas import tpu as pltpu
from jax.sharding import PartitionSpec as P

DH = 128
GROUP = 4
TOPK = 3
LOG2E = 1.4426950408889634
LOW = -3e38
SCALE = DH ** (-0.5) * LOG2E
VMEM = 16 << 20
CROSSES = ((1, 1, 1, 1), (0, 1, 0, 0), (1, 0, 0, 0))


def own(place, head):
    return 0, 0


def across(place, head):
    return 3, place // GROUP & 1


def lane(place, head):
    return head ^ ((place ^ place >> 1) & 1)


def beside(place, head):
    return 1 + lane(place, head), 1


def other_beside(place, head):
    return 2 - lane(place, head), 1


def other_core(place, head):
    return 0, 1


def block_away(step, place, head):
    lower = min(place, place ^ step * GROUP) // GROUP
    return step * GROUP, CROSSES[min(step, 3) - 1][lower & 3]


def swapped(rows, route):
    seq, head = lax.axis_size("seq"), lax.axis_size("head")
    pairs = []
    for i in range(seq):
        for h in range(head):
            step, flip = route(i, h)
            pairs.append((i * head + h, (i ^ step) * head + (h ^ flip)))
    return lax.ppermute(rows, ("seq", "head"), pairs)


def kernel_call(body, out_shape, name, arrays):
    vmem = pl.BlockSpec(memory_space=pltpu.VMEM)
    return pl.pallas_call(
        body,
        out_shape=out_shape,
        in_specs=[vmem] * len(arrays),
        out_specs=jax.tree.map(lambda _: vmem, out_shape),
        compiler_params=pltpu.CompilerParams(vmem_limit_bytes=VMEM),
        name=name,
    )(*arrays)


def join_kernel(*refs):
    rows = refs[0].shape[0]
    for index, piece in enumerate(refs[:-1]):
        refs[-1][index * rows : (index + 1) * rows, :] = piece[...]


def join(pieces):
    rows, width = pieces[0].shape
    out = jax.ShapeDtypeStruct((len(pieces) * rows, width), pieces[0].dtype)
    return kernel_call(join_kernel, out, "join", pieces)


def plan_kernel(selected_ref, wanted_ref):
    me = lax.axis_index("seq")
    for index, route in enumerate((own, across, beside, other_beside)):
        step, _ = route(me, lax.axis_index("head"))
        for column in range(1, TOPK):
            wanted = selected_ref[pl.ds(me ^ step, 1), column : column + 1] ^ (me // GROUP)
            row = index * (TOPK - 1) + column - 1
            wanted_ref[row : row + 1, :] = jnp.broadcast_to(wanted, (1, DH))


def pick_kernel(columns, blocks, wanted_ref, *refs):
    held, messages = refs[:blocks], refs[blocks:]
    rows = held[0].shape[0]
    for index in range(GROUP):
        messages[index][0:rows, :] = held[0][...]
        for column in range(1, columns):
            picked = held[1][...]
            if columns > 2:
                row = index * (TOPK - 1) + column - 1
                wanted = jnp.broadcast_to(wanted_ref[row : row + 1, :], (rows, DH))
                wanted = jnp.concatenate([wanted, wanted], axis=1)
                for other in range(2, blocks):
                    picked = jnp.where(wanted == other, held[other][...], picked)
            messages[index][column * rows : (column + 1) * rows, :] = picked


def pick(columns, selected, held):
    rows, width = held[0].shape
    messages = [jax.ShapeDtypeStruct((columns * rows, width), held[0].dtype)] * GROUP
    body = functools.partial(pick_kernel, columns, len(held))
    return kernel_call(body, messages, f"pick_{columns}", [selected, *held])


def attend_kernel(rows, places, resumed, last, queries_ref, *refs):
    pieces, rest = refs[: len(places)], refs[len(places) :]
    state, outs = (rest[:3], rest[3:]) if resumed else ((), rest)
    tokens, width = queries_ref.shape
    heads = width // DH
    me = lax.axis_index("seq")
    head = lax.axis_index("head")
    queries = queries_ref[...]
    stacked = jnp.concatenate([queries[:, h * DH : (h + 1) * DH] for h in range(heads)], axis=0)
    parts = [piece[:rows, :] for piece in pieces]
    parts += [piece[rows:, :] for piece in pieces if piece.shape[0] > rows]
    kv = jnp.concatenate(parts, axis=0)
    scores = lax.dot_general(
        stacked, kv[:, :DH], (((1,), (1,)), ((), ())), preferred_element_type=jnp.float32
    )
    edge = min(-(-len(pieces) * rows // DH) * DH, kv.shape[0])
    lane = lax.broadcasted_iota(jnp.int32, (1, edge), 1)
    position = jnp.zeros_like(lane)
    for index, (route, relayed) in enumerate(places):
        step, flip = route(me, head ^ relayed)
        start = ((me ^ step) % GROUP) * tokens + (head ^ relayed ^ flip) * rows - index * rows
        inside = (lane >= index * rows) & (lane < (index + 1) * rows)
        position = jnp.where(inside, start + lane, position)
    token = lax.broadcasted_iota(jnp.int32, (heads * tokens, 1), 0) % tokens
    own = jnp.where(position <= (me % GROUP) * tokens + token, scores[:, :edge], LOW)
    scores = jnp.concatenate([own, scores[:, edge:]], axis=1) if edge < kv.shape[0] else own
    top = jnp.broadcast_to(jnp.max(scores, axis=1, keepdims=True), (heads * tokens, DH))
    if resumed:
        before = state[0][...]
        top = jnp.maximum(top, before)
    columns = [scores[:, start : start + DH] for start in range(0, scores.shape[1], DH)]
    weights = jnp.concatenate([jnp.exp2((c - top[:, : c.shape[1]]) * SCALE).astype(jnp.bfloat16) for c in columns], axis=1)
    values = jnp.concatenate([kv[:, DH:], jnp.ones_like(kv[:, DH:])], axis=1)
    sums = jnp.dot(weights, values, preferred_element_type=jnp.float32)
    out, total = sums[:, :DH], sums[:, DH:]
    if resumed:
        scale = jnp.exp2((before - top) * SCALE)
        total += scale * state[1][...]
        out += scale * state[2][...]
    if not last:
        outs[0][...] = top
        outs[1][...] = total
        outs[2][...] = out
        return
    out /= total
    for h in range(heads):
        outs[0][:, h * DH : (h + 1) * DH] = out[h * tokens : (h + 1) * tokens].astype(outs[0].dtype)


def attend(rows, queries, placed, state=(), last=True):
    tokens, width = queries.shape
    running = jax.ShapeDtypeStruct((tokens * width // DH, DH), jnp.float32)
    out = jax.ShapeDtypeStruct(queries.shape, queries.dtype) if last else [running] * 3
    places, pieces = zip(*placed)
    body = functools.partial(attend_kernel, rows, places, bool(state), last)
    return kernel_call(body, out, f"attend_{len(pieces)}", [queries, *pieces, *state])


def first_block(queries, rows):
    diagonal = swapped(rows, across)
    first = swapped(rows, beside)
    diagonal, again = lax.optimization_barrier((diagonal, rows))
    near = join([rows, first, swapped(again, other_beside), diagonal])
    far = swapped(near, other_core)
    length = rows.shape[0]
    placed = []
    for relayed, piece in enumerate((near, far)):
        for index, route in enumerate((own, beside, other_beside, across)):
            placed.append(((route, relayed), piece[index * length : (index + 1) * length]))
    return attend(length, queries, placed)


def later_block(columns, queries, selected, held):
    length = held[0].shape[0]
    messages = pick(columns, selected, held)
    near = [messages[0]] + [swapped(m, route) for m, route in zip(messages[1:], (across, beside, other_beside))]
    far = [swapped(piece, other_core) for piece in near]
    placed = [((own, 0), near[0]), ((own, 1), far[0]), ((across, 0), near[1]), ((across, 1), far[1]), ((beside, 0), near[2]), ((other_beside, 0), near[3])]
    state = attend(length, queries, placed, last=False)
    placed = [((beside, 1), far[2]), ((other_beside, 1), far[3])]
    return attend(length, queries, placed, state)


def shards(queries, keys_values, selected):
    blocks = lax.axis_size("seq") // GROUP
    mine = lax.axis_index("seq") // GROUP
    held = {0: keys_values}
    for step in range(blocks - 1, 0, -1):
        held[step] = swapped(keys_values, functools.partial(block_away, step))
    held = [held[step] for step in range(blocks)]
    held[2], held[1] = lax.optimization_barrier((held[2], held[1]))
    held[3], held[2] = lax.optimization_barrier((held[3], held[2]))
    selected = kernel_call(plan_kernel, jax.ShapeDtypeStruct((2 * GROUP, DH), jnp.int32), "plan", [selected])
    level = jnp.minimum(mine, TOPK - 1)
    first = lax.cond(
        level == 0,
        lambda: first_block(queries, keys_values),
        lambda: jnp.zeros_like(queries),
    )
    branches = [functools.partial(later_block, columns) for columns in range(2, TOPK + 1)]
    return lax.switch(level, [lambda *_: first] + branches, queries, selected, held)


def solution(mesh):
    in_specs = (P("seq", "head"), P(("seq", "head"), None), P())
    out_specs = P("seq", "head")
    return jax.shard_map(shards, mesh=mesh, in_specs=in_specs, out_specs=out_specs, check_vma=False)
```
